32 devices in a mesh: clip: 4 (over y, x), seq: 8 (over z, core).
Axes of the slice: x: 2, y: 2, z: 4, core: 2. Of those that a mesh axis runs over, the one named last changes fastest.
Arguments:
- queries: bfloat16 [16384, 1024], P(('clip', 'seq')), parts along dimension 0, may hold values from -50 to 50
- rgb_kv: bfloat16 [8, 4096, 1024], P('clip', 'seq'), parts along dimension 0, may hold values from -16 to 16
- tile_ids: int32 [128, 8], P(('clip', 'seq')), parts along dimension 0, may hold values from 0 to 31, as said below
- tile_count: int32 [128], P(('clip', 'seq')), parts along dimension 0, may hold values from 2 to 8
- out_weight: bfloat16 [1024, 1024], replicated, may hold values from -0.1875 to 0.1875
- out_grad: bfloat16 [16384, 1024], P(('clip', 'seq')), parts along dimension 0, may hold values from -6 to 6
Outputs:
- joined: bfloat16 [16384, 1024], P(('clip', 'seq')), parts along dimension 0
- d_queries: bfloat16 [16384, 1024], P(('clip', 'seq')), parts along dimension 0
- d_kv: bfloat16 [8, 4096, 1024], P('clip', 'seq'), parts along dimension 0
- d_out_weight: float32 [4096, 1024], P(('clip', 'seq')), parts along dimension 0
The draws below stay inside these ranges and needn't reach their ends.
There are 4 independent parts, one for each index of `clip`. The reference program is written for one: setup_inputs(seed, part) draws one part's arguments, and reference() takes and returns one part's arrays. A program takes and returns all parts, laid end to end along the dimension named above; an argument that names none is the same for every part. Nothing has to cross between parts.
Inputs may be any that keep to these rules, and one draw needn't show every extreme that they name: `tile_ids`: the 4 consecutive blocks of one group name, in their live entries, at most one distinct tile among tiles 4 s to 4 s + 3, for every s. The entries of one list name distinct tiles.
All inputs are finite; a program needn't handle non-finite values.
Results may differ from the reference program's by a relative error of at most 0.015.
Values may be sent and summed in bfloat16 or wider, within the bound.
A program may use at most 192 MiB of HBM per device.

```python
import jax
import jax.numpy as jnp
from jax import lax

D = 1024
HEADS = 16
EB = 128
TILE = 128
KMAX = 8
EBLK_DEV = 4
TILE_DEV = 4
NBLK = 32
TOKENS = 4096
NTILE = 32
RGB_TOK = 4096


def block_tables(key):
    sources = NTILE // TILE_DEV
    key_local, key_order, key_count = jax.random.split(jax.random.fold_in(key, 11), 3)
    local_choice = jax.random.randint(key_local, (sources, sources), 0, TILE_DEV)
    ranking = jax.random.randint(key_order, (NBLK, sources), 0, 1 << 20) * sources + jnp.arange(sources)[None, :]
    chosen_sources = jnp.argsort(ranking, axis=1)[:, :KMAX].astype(jnp.int32)
    owner_group = jnp.arange(NBLK) // EBLK_DEV
    chosen_local = jnp.take_along_axis(local_choice[owner_group], chosen_sources, axis=1)
    tile_table = chosen_sources * TILE_DEV + chosen_local
    counts = jax.random.randint(key_count, (NBLK,), 2, KMAX + 1)
    counts = counts.at[0].set(KMAX).at[1].set(2)
    return (tile_table.astype(jnp.int32), counts.astype(jnp.int32))


def float_fields(key):
    parts_list = jax.random.split(jax.random.fold_in(key, 23), 5)
    query_field = jnp.clip(1.2 * jax.random.normal(parts_list[1], (TOKENS, D)), -6.0, 6.0)
    key_field = jnp.clip(1.2 * jax.random.normal(parts_list[3], (RGB_TOK, D)), -6.0, 6.0)
    value_field = jnp.clip(3.0 * jax.random.normal(parts_list[4], (RGB_TOK, D)), -16.0, 16.0)
    return (query_field, key_field, value_field)


def draw_queries(key, part):
    return float_fields(key)[0].astype(jnp.bfloat16)


def draw_rgb_kv(key, part):
    fields = float_fields(key)
    return jnp.stack([fields[1], fields[2]]).astype(jnp.bfloat16)


def draw_tile_ids(key, part):
    return block_tables(key)[0]


def draw_tile_count(key, part):
    return block_tables(key)[1]


def spiked(drawn, key, source, target, shards_of, factor):
    owner, partner = [(jnp.arange(drawn.shape[dim]) // (drawn.shape[dim] // shards_of)).reshape([-1 if axis == dim else 1 for axis in range(drawn.ndim)]) for dim in (source, target)]
    chosen = jax.random.permutation(key, shards_of)[partner]
    strong = (owner == chosen) | (owner == (partner + shards_of // 2) % shards_of)
    return jnp.where(strong, factor * drawn, drawn)


def levels(stream_key, extent, cuts, smallest, largest):
    def one(axis_at, shards_of):
        draws = jax.random.uniform(jax.random.fold_in(jax.random.fold_in(stream_key, 6), axis_at), (shards_of,), jnp.float32, smallest / len(cuts), largest / len(cuts))
        return jnp.repeat(jnp.exp(draws), extent[axis_at] // shards_of).reshape((-1,) + (1,) * (len(extent) - axis_at - 1))

    gain = one(*cuts[0])
    for cut in cuts[1:]:
        gain = gain * one(*cut)
    return gain


def normal_values(own_key, shape, width, most, shards=(), held_as=jnp.bfloat16):
    drawn = jax.random.normal(own_key, shape, jnp.float32) * width
    if len(shards) > 0:
        drawn = levels(own_key, shape, shards, -0.22, 0.18) * drawn
    return jnp.clip(drawn, min=-most, max=most).astype(held_as)


def noise_with(own_key, shape, spread, most, cuts, heavy, held_as=jnp.bfloat16):
    result = spread * jax.random.normal(own_key, shape, jnp.float32)
    if cuts:
        result = result * levels(own_key, shape, cuts, -0.22, 0.18)
    return jnp.clip(spiked(result, jax.random.fold_in(own_key, 3), *heavy), -most, most).astype(held_as)


def setup_inputs(seed: int = 0, part: int = 0) -> dict:
    seeds = jax.random.split(jax.random.key(seed), 7)
    own_keys = jax.random.split(jax.random.fold_in(seeds[6], part), 7)
    queries = draw_queries(jax.random.fold_in(jax.random.fold_in(seeds[6], part), 71), part)
    rgb_kv = draw_rgb_kv(jax.random.fold_in(jax.random.fold_in(seeds[6], part), 71), part)
    tile_ids = draw_tile_ids(jax.random.fold_in(jax.random.fold_in(seeds[6], part), 71), part)
    tile_count = draw_tile_count(jax.random.fold_in(jax.random.fold_in(seeds[6], part), 71), part)
    out_weight = normal_values(seeds[4], (D, D), D ** -0.5, 0.1875)
    out_grad = noise_with(own_keys[5], (TOKENS, D), 1.0, 6.0, ((0, 8),), (0, 1, 8, 2.0))
    return dict(queries=queries, rgb_kv=rgb_kv, tile_ids=tile_ids, tile_count=tile_count, out_weight=out_weight, out_grad=out_grad)


masked_score = -1.0e30


def rounded(values):
    return lax.optimization_barrier(values.astype(jnp.bfloat16))


def reference(queries, rgb_kv, tile_ids, tile_count, out_weight, out_grad):
    sources = NTILE // TILE_DEV
    head_dim = D // HEADS
    score_scale = head_dim ** -0.5
    tile_rows = rgb_kv.reshape(2, NTILE, TILE, D)
    group_queries = queries.reshape(sources, EBLK_DEV, EB, HEADS, head_dim)
    group_ids = tile_ids.reshape(sources, EBLK_DEV, KMAX)
    group_count = tile_count.reshape(sources, EBLK_DEV)
    group_grad = out_grad.reshape(sources, EBLK_DEV * EB, D)

    def one_group(running, inputs):
        query_heads, id_rows, count_rows, grad_rows = inputs
        query_float = query_heads.astype(jnp.float32)
        usable = jnp.arange(KMAX)[None, :] < count_rows[:, None]
        key_rows = tile_rows[0][id_rows].reshape(EBLK_DEV, KMAX * TILE, HEADS, head_dim).astype(jnp.float32)
        value_rows = tile_rows[1][id_rows].reshape(EBLK_DEV, KMAX * TILE, HEADS, head_dim).astype(jnp.float32)
        key_usable = jnp.repeat(usable, TILE, axis=1)
        logits = jnp.einsum("bqhe,bthe->bhqt", query_float, key_rows) * score_scale
        logits = jnp.where(key_usable[:, None, None, :], logits, masked_score)
        row_max = jnp.max(logits, axis=3, keepdims=True)
        row_sum = jnp.sum(jnp.exp(logits - row_max), axis=3, keepdims=True)
        probability = jnp.exp(logits - row_max) / row_sum
        weights = rounded(probability).astype(jnp.float32)
        attended_full = jnp.einsum("bhqt,bthe->bqhe", weights, value_rows)
        attended = rounded(attended_full).reshape(EBLK_DEV * EB, D)
        joined_out = jnp.dot(attended, out_weight, preferred_element_type=jnp.float32).astype(jnp.bfloat16)
        d_attended = rounded(lax.dot_general(grad_rows, out_weight, (((1,), (1,)), ((), ())), preferred_element_type=jnp.float32))
        d_heads = d_attended.reshape(EBLK_DEV, EB, HEADS, head_dim).astype(jnp.float32)
        delta_rows = jnp.sum(d_heads * attended_full, axis=3).transpose(0, 2, 1)[..., None]
        d_weights = jnp.einsum("bqhe,bthe->bhqt", d_heads, value_rows)
        d_scores = rounded(probability * (d_weights - delta_rows)).astype(jnp.float32)
        d_query = (jnp.einsum("bhqt,bthe->bqhe", d_scores, key_rows) * score_scale).astype(jnp.bfloat16)
        d_keys = jnp.einsum("bhqt,bqhe->bthe", d_scores, query_float) * score_scale
        d_values = jnp.einsum("bhqt,bqhe->bthe", weights, d_heads)
        source = id_rows // TILE_DEV
        within = id_rows % TILE_DEV
        matches = (source[:, :, None] == jnp.arange(sources)[None, None, :]) & usable[:, :, None]
        slot_terms = jnp.stack([d_keys.reshape(EBLK_DEV, KMAX, TILE, D), d_values.reshape(EBLK_DEV, KMAX, TILE, D)])
        slot_sums = jnp.einsum("bks,cbktd->cstd", matches.astype(jnp.float32), slot_terms)
        group_terms = rounded(slot_sums).astype(jnp.float32)
        owner_pick = jnp.any(matches[:, :, :, None] & (within[:, :, None, None] == jnp.arange(TILE_DEV)[None, None, None, :]), axis=(0, 1))
        running = running + jnp.einsum("sl,cstd->csltd", owner_pick.astype(jnp.float32), group_terms)
        return running, (joined_out, d_query.reshape(EBLK_DEV * EB, D), attended)

    start = jnp.zeros((2, sources, TILE_DEV, TILE, D), jnp.float32)
    running, outputs = lax.scan(one_group, start, (group_queries, group_ids, group_count, group_grad))
    joined_all, d_query_all, attended_all = outputs
    attended_all = attended_all.reshape(TOKENS, D)
    d_out_weight = jnp.dot(attended_all.T, out_grad, preferred_element_type=jnp.float32)
    d_kv = running.reshape(2, RGB_TOK, D).astype(jnp.bfloat16)
    return joined_all.reshape(TOKENS, D), d_query_all.reshape(TOKENS, D), d_kv, d_out_weight
```

```python
import functools

import jax
import jax.numpy as jnp
from jax import lax
from jax.experimental import pallas as pl
from jax.experimental.pallas import tpu as pltpu
from jax.sharding import PartitionSpec as P

D = 1024
HEADS = 16
EB = 128
TILE = 128
HEAD_DIM = D // HEADS
PAIR = 2 * HEAD_DIM
CHUNKS = (2, 2, 2, 2)
UNROLL = 2
VMEM_LIMIT = 48 * 1024 * 1024

masked_score = -1e30


def entry_tables(tile_ids, tile_count, tiles_dev, sources):
    entries = tile_ids.shape[1]
    source = tile_ids // tiles_dev
    within = tile_ids % tiles_dev
    usable = jnp.arange(entries)[None, :] < tile_count[:, None]
    matches = (source[:, :, None] == jnp.arange(sources)[None, None, :]) & usable[:, :, None]
    needed = jnp.any(matches, axis=(0, 1))
    wanted = jnp.max(jnp.where(matches, within[:, :, None], 0), axis=(0, 1))
    request = jnp.where(needed, wanted, -1)
    return (source, request)


def gather_kernel(asked_ref, tiles_ref, out_ref):
    out_ref[0] = tiles_ref[:, 0]


def gather_tiles(asked, tiles, first, pairs):
    sources = asked.shape[0]
    width = pairs * PAIR
    return pl.pallas_call(
        gather_kernel,
        grid_spec=pltpu.PrefetchScalarGridSpec(
            num_scalar_prefetch=1,
            grid=(sources,),
            in_specs=[
                pl.BlockSpec(
                    (2, 1, TILE, width),
                    lambda s, asked_ref: (0, jnp.maximum(asked_ref[s], 0), 0, first // pairs),
                )
            ],
            out_specs=pl.BlockSpec((1, 2, TILE, width), lambda s, asked_ref: (s, 0, 0, 0)),
        ),
        out_shape=jax.ShapeDtypeStruct((sources, 2, TILE, width), jnp.bfloat16),
        compiler_params=pltpu.CompilerParams(vmem_limit_bytes=VMEM_LIMIT),
        cost_estimate=pl.CostEstimate(
            flops=0, bytes_accessed=sources * TILE * width * 8, transcendentals=0
        ),
    )(asked, tiles)


def sum_kernel(asked_ref, terms_ref, *rest):
    out_ref, acc = rest[-2:]
    sources = terms_ref.shape[0]
    acc[...] = jnp.zeros_like(acc)

    def step(s, carry):
        asked = asked_ref[s]

        @pl.when(asked >= 0)
        def _():
            for c in range(2):
                acc[c, asked] += terms_ref[s, c].astype(jnp.float32)

        return carry

    lax.fori_loop(0, sources, step, 0)
    out_ref[...] = acc[...].astype(jnp.bfloat16)


def sum_terms(asked, terms, held, tiles_dev, first, pairs):
    sources = asked.shape[0]
    specs = [
        pl.BlockSpec((sources, 2, TILE, PAIR), lambda p, asked_ref: (0, 0, 0, p)),
    ]
    operands = [asked, terms]
    aliases = {}
    if held is not None:
        specs.append(pl.BlockSpec(memory_space=pl.ANY))
        operands.append(held)
        aliases = {2: 0}
    return pl.pallas_call(
        sum_kernel,
        grid_spec=pltpu.PrefetchScalarGridSpec(
            num_scalar_prefetch=1,
            grid=(pairs,),
            in_specs=specs,
            out_specs=pl.BlockSpec(
                (2, tiles_dev, TILE, PAIR), lambda p, asked_ref: (0, 0, 0, first + p)
            ),
            scratch_shapes=[pltpu.VMEM((2, tiles_dev, TILE, PAIR), jnp.float32)],
        ),
        out_shape=jax.ShapeDtypeStruct((2, tiles_dev, TILE, D), jnp.bfloat16),
        input_output_aliases=aliases,
        compiler_params=pltpu.CompilerParams(vmem_limit_bytes=VMEM_LIMIT),
        cost_estimate=pl.CostEstimate(
            flops=sources * TILE * pairs * PAIR * 2,
            bytes_accessed=sources * TILE * pairs * PAIR * 6,
            transcendentals=0,
        ),
    )(*operands)


def dot(a, b):
    return jnp.dot(a, b, preferred_element_type=jnp.float32)


def by_head(transposed):
    row = lax.broadcasted_iota(jnp.int32, (PAIR, EB), 0)
    return jnp.where(row < HEAD_DIM, transposed[:, :EB], transposed[:, EB:])


def attention_kernel(source_ref, count_ref, q_ref, da_ref, kv_ref, *rest):
    att_ref, dq_ref, grads_ref, flipped, scores, sums, qm, qmt, dm, dmt, out_t, dq_t = rest[-12:]
    sources = kv_ref.shape[0]
    blocks = q_ref.shape[0] // EB
    rows_now = UNROLL * TILE
    lane = lax.broadcasted_iota(jnp.int32, (EB, PAIR), 1)
    row = lax.broadcasted_iota(jnp.int32, (PAIR, EB), 0)

    def flip(s, carry):
        for c in range(2):
            flipped[s, c] = kv_ref[s, c].T
        sums[s] = jnp.zeros((2, TILE, PAIR), jnp.float32)
        return carry

    lax.fori_loop(0, sources, flip, 0)

    def spread(block, natural, turned):
        zero = jnp.zeros((EB, PAIR), jnp.bfloat16)
        natural[:EB, :] = jnp.where(lane < HEAD_DIM, block, zero)
        natural[EB:, :] = jnp.where(lane >= HEAD_DIM, block, zero)
        block_t = block.T
        turned[:, :EB] = jnp.where(row < HEAD_DIM, block_t, zero)
        turned[:, EB:] = jnp.where(row >= HEAD_DIM, block_t, zero)

    def one_block(b, carry):
        here = pl.ds(pl.multiple_of(b * EB, EB), EB)
        spread(q_ref[here, :] * jnp.bfloat16(HEAD_DIM**-0.5), qm, qmt)
        spread(da_ref[here, :], dm, dmt)
        count = count_ref[b]
        trips = (count + UNROLL - 1) // UNROLL

        def rows_of(trip):
            return pl.ds(pl.multiple_of(trip * rows_now, rows_now), rows_now)

        def slots_of(trip):
            return [source_ref[b, trip * UNROLL + u] for u in range(UNROLL)]

        def score_step(trip, top):
            for u, slot in enumerate(slots_of(trip)):
                entry = trip * UNROLL + u
                logits = jnp.where(entry < count, dot(kv_ref[slot, 0], qmt[...]), masked_score)
                at = pl.ds(pl.multiple_of(entry * TILE, TILE), TILE)
                scores[at, :] = logits
                top = jnp.maximum(top, jnp.max(logits.reshape(TILE // 8, 8, 2 * EB), axis=0))
            return top

        top = lax.fori_loop(
            0, trips, score_step, jnp.full((8, 2 * EB), masked_score, jnp.float32)
        )
        row_max = jnp.max(top, axis=0, keepdims=True)
        out_t[...] = jnp.zeros_like(out_t)

        def output_step(trip, total):
            at = rows_of(trip)
            terms = jnp.exp(scores[at, :] - row_max)
            scores[at, :] = terms
            values = jnp.concatenate([flipped[s, 1] for s in slots_of(trip)], axis=1)
            out_t[...] += dot(values, terms.astype(jnp.bfloat16))
            return total + jnp.sum(terms.reshape(rows_now // 8, 8, 2 * EB), axis=0)

        total = lax.fori_loop(0, trips, output_step, jnp.zeros((8, 2 * EB), jnp.float32))
        inverse = 1.0 / jnp.sum(total, axis=0, keepdims=True)
        full = out_t[...] * inverse
        att_ref[here, :] = by_head(full).T.astype(jnp.bfloat16)
        delta = jnp.sum(full * dmt[...].astype(jnp.float32), axis=0, keepdims=True)
        dq_t[...] = jnp.zeros_like(dq_t)

        def grad_step(trip, carry):
            at = rows_of(trip)
            slots = slots_of(trip)
            probability = scores[at, :] * inverse
            values = jnp.concatenate([kv_ref[s, 1] for s in slots], axis=0)
            d_weights = dot(values, dmt[...])
            d_scores = (probability * (d_weights - delta)).astype(jnp.bfloat16)
            keys_t = jnp.concatenate([flipped[s, 0] for s in slots], axis=1)
            dq_t[...] += dot(keys_t, d_scores)
            d_keys = dot(d_scores, qm[...])
            d_values = dot(probability.astype(jnp.bfloat16), dm[...])
            for u, slot in enumerate(slots):
                sums[slot, 0] += d_keys[u * TILE : (u + 1) * TILE]
                sums[slot, 1] += d_values[u * TILE : (u + 1) * TILE]
            return carry

        lax.fori_loop(0, trips, grad_step, 0)
        dq_ref[here, :] = (by_head(dq_t[...]).T * HEAD_DIM**-0.5).astype(jnp.bfloat16)
        return carry

    lax.fori_loop(0, blocks, one_block, 0)

    def finish(s, carry):
        grads_ref[s] = sums[s].astype(jnp.bfloat16)
        return carry

    lax.fori_loop(0, sources, finish, 0)


def attention(source, count, queries, d_attended, slots, held, first, pairs):
    sources = slots.shape[0]
    tokens = queries.shape[0]
    entries = source.shape[1]
    columns = pl.BlockSpec((tokens, PAIR), lambda p, *_: (0, first + p))
    chunk = pl.BlockSpec((sources, 2, TILE, PAIR), lambda p, *_: (0, 0, 0, p))
    specs = [columns, columns, chunk]
    operands = [source, count, queries, d_attended, slots]
    aliases = {}
    if held is not None:
        specs += [pl.BlockSpec(memory_space=pl.ANY)] * 2
        operands += list(held)
        aliases = {5: 0, 6: 1}
    whole = jax.ShapeDtypeStruct((tokens, D), jnp.bfloat16)
    products = (tokens // EB) * entries * pairs * TILE * 2 * EB * PAIR * 2 * 6
    return pl.pallas_call(
        attention_kernel,
        grid_spec=pltpu.PrefetchScalarGridSpec(
            num_scalar_prefetch=2,
            grid=(pairs,),
            in_specs=specs,
            out_specs=[columns, columns, chunk],
            scratch_shapes=[
                pltpu.VMEM((sources, 2, TILE, PAIR), jnp.bfloat16),
                pltpu.VMEM((entries * TILE, 2 * EB), jnp.float32),
                pltpu.VMEM((sources, 2, TILE, PAIR), jnp.float32),
                pltpu.VMEM((2 * EB, PAIR), jnp.bfloat16),
                pltpu.VMEM((PAIR, 2 * EB), jnp.bfloat16),
                pltpu.VMEM((2 * EB, PAIR), jnp.bfloat16),
                pltpu.VMEM((PAIR, 2 * EB), jnp.bfloat16),
                pltpu.VMEM((PAIR, 2 * EB), jnp.float32),
                pltpu.VMEM((PAIR, 2 * EB), jnp.float32),
            ],
        ),
        out_shape=[
            whole,
            whole,
            jax.ShapeDtypeStruct((sources, 2, TILE, pairs * PAIR), jnp.bfloat16),
        ],
        input_output_aliases=aliases,
        compiler_params=pltpu.CompilerParams(vmem_limit_bytes=VMEM_LIMIT),
        cost_estimate=pl.CostEstimate(
            flops=products * 4, bytes_accessed=sources * TILE * pairs * PAIR * 8, transcendentals=0
        ),
    )(*operands)


def exchange(array):
    return lax.all_to_all(array, "seq", split_axis=0, concat_axis=0, tiled=True)


def token_sum(partial, sources):
    core = lax.axis_index("seq") % 2
    parts = partial.reshape(sources // 2, 2, partial.shape[0] // sources, D)
    kept = lax.dynamic_index_in_dim(parts, core, 1, keepdims=False)
    given = lax.dynamic_index_in_dim(parts, 1 - core, 1, keepdims=False).astype(jnp.bfloat16)
    got = lax.ppermute(given, "seq", [(i, i ^ 1) for i in range(sources)])
    chip = (kept + got.astype(jnp.float32)).astype(jnp.bfloat16)
    groups = [list(range(c, sources, 2)) for c in range(2)]
    terms = lax.all_to_all(
        chip, "seq", split_axis=0, concat_axis=0, tiled=True, axis_index_groups=groups
    )
    return jnp.sum(terms.astype(jnp.float32), axis=0)


def local(queries, rgb_kv, tile_ids, tile_count, out_weight, out_grad):
    sources = lax.axis_size("seq")
    tiles_dev = rgb_kv.shape[1] // TILE
    source, request = entry_tables(tile_ids, tile_count, tiles_dev, sources)
    asked = exchange(request[:, None])[:, 0]
    tiles = rgb_kv.reshape(2, tiles_dev, TILE, D)
    starts = [sum(CHUNKS[:i]) for i in range(len(CHUNKS))]
    cuts = list(zip(starts, CHUNKS))
    fetched = [exchange(gather_tiles(asked, tiles, first, pairs)) for first, pairs in cuts]
    d_attended = lax.dot_general(
        out_grad, out_weight, (((1,), (1,)), ((), ())), preferred_element_type=jnp.float32
    ).astype(jnp.bfloat16)
    held = None
    returned = []
    for (first, pairs), slots in zip(cuts, fetched):
        attended, d_queries, grads = attention(
            source, tile_count, queries, d_attended, slots, held, first, pairs
        )
        held = (attended, d_queries)
        returned.append(exchange(grads))
    partial = lax.dot_general(
        attended, out_grad, (((0,), (0,)), ((), ())), preferred_element_type=jnp.float32
    )
    d_out_weight = token_sum(partial, sources)
    joined = dot(attended, out_weight).astype(jnp.bfloat16)
    d_kv = None
    for (first, pairs), terms in zip(cuts, returned):
        d_kv = sum_terms(asked, terms, d_kv, tiles_dev, first, pairs)
    return (joined, d_queries, d_kv.reshape(2, tiles_dev * TILE, D), d_out_weight)


def solution(mesh):
    placed = (
        P(("clip", "seq"), None),
        P("clip", "seq", None),
        P(("clip", "seq"), None),
        P(("clip", "seq")),
        P(),
        P(("clip", "seq"), None),
    )
    return jax.shard_map(
        local,
        mesh=mesh,
        in_specs=placed,
        out_specs=(
            P(("clip", "seq"), None),
            P(("clip", "seq"), None),
            P("clip", "seq", None),
            P(("clip", "seq"), None),
        ),
        check_vma=False,
    )
```

```python
import functools

import jax
import jax.numpy as jnp
from jax import lax
from jax.experimental import pallas as pl
from jax.experimental.pallas import tpu as pltpu
from jax.sharding import PartitionSpec as P

D = 1024
HEADS = 16
EB = 128
TILE = 128
HEAD_DIM = D // HEADS
PAIR = 2 * HEAD_DIM
CHUNKS = (4, 4)
UNROLL = 2
VMEM_LIMIT = 48 * 1024 * 1024

masked_score = -1e30


def entry_tables(tile_ids, tile_count, tiles_dev, sources):
    entries = tile_ids.shape[1]
    source = tile_ids // tiles_dev
    within = tile_ids % tiles_dev
    usable = jnp.arange(entries)[None, :] < tile_count[:, None]
    matches = (source[:, :, None] == jnp.arange(sources)[None, None, :]) & usable[:, :, None]
    needed = jnp.any(matches, axis=(0, 1))
    wanted = jnp.max(jnp.where(matches, within[:, :, None], 0), axis=(0, 1))
    request = jnp.where(needed, wanted, -1)
    return (source, request)


def gather_kernel(asked_ref, tiles_ref, out_ref):
    out_ref[0] = tiles_ref[:, 0]


def gather_tiles(asked, tiles, first, pairs):
    sources = asked.shape[0]
    width = pairs * PAIR
    return pl.pallas_call(
        gather_kernel,
        grid_spec=pltpu.PrefetchScalarGridSpec(
            num_scalar_prefetch=1,
            grid=(sources,),
            in_specs=[
                pl.BlockSpec(
                    (2, 1, TILE, width),
                    lambda s, asked_ref: (0, jnp.maximum(asked_ref[s], 0), 0, first // pairs),
                )
            ],
            out_specs=pl.BlockSpec((1, 2, TILE, width), lambda s, asked_ref: (s, 0, 0, 0)),
        ),
        out_shape=jax.ShapeDtypeStruct((sources, 2, TILE, width), jnp.bfloat16),
        compiler_params=pltpu.CompilerParams(vmem_limit_bytes=VMEM_LIMIT),
        cost_estimate=pl.CostEstimate(
            flops=0, bytes_accessed=sources * TILE * width * 8, transcendentals=0
        ),
    )(asked, tiles)


def sum_kernel(asked_ref, terms_ref, *rest):
    out_ref, acc = rest[-2:]
    sources = terms_ref.shape[0]
    acc[...] = jnp.zeros_like(acc)

    def step(s, carry):
        asked = asked_ref[s]

        @pl.when(asked >= 0)
        def _():
            for c in range(2):
                acc[c, asked] += terms_ref[s, c].astype(jnp.float32)

        return carry

    lax.fori_loop(0, sources, step, 0)
    out_ref[...] = acc[...].astype(jnp.bfloat16)


def sum_terms(asked, terms, held, tiles_dev, first, pairs):
    sources = asked.shape[0]
    specs = [
        pl.BlockSpec((sources, 2, TILE, PAIR), lambda p, asked_ref: (0, 0, 0, p)),
    ]
    operands = [asked, terms]
    aliases = {}
    if held is not None:
        specs.append(pl.BlockSpec(memory_space=pl.ANY))
        operands.append(held)
        aliases = {2: 0}
    return pl.pallas_call(
        sum_kernel,
        grid_spec=pltpu.PrefetchScalarGridSpec(
            num_scalar_prefetch=1,
            grid=(pairs,),
            in_specs=specs,
            out_specs=pl.BlockSpec(
                (2, tiles_dev, TILE, PAIR), lambda p, asked_ref: (0, 0, 0, first + p)
            ),
            scratch_shapes=[pltpu.VMEM((2, tiles_dev, TILE, PAIR), jnp.float32)],
        ),
        out_shape=jax.ShapeDtypeStruct((2, tiles_dev, TILE, D), jnp.bfloat16),
        input_output_aliases=aliases,
        compiler_params=pltpu.CompilerParams(vmem_limit_bytes=VMEM_LIMIT),
        cost_estimate=pl.CostEstimate(
            flops=sources * TILE * pairs * PAIR * 2,
            bytes_accessed=sources * TILE * pairs * PAIR * 6,
            transcendentals=0,
        ),
    )(*operands)


def dot(a, b):
    return jnp.dot(a, b, preferred_element_type=jnp.float32)


def by_head(transposed):
    row = lax.broadcasted_iota(jnp.int32, (PAIR, EB), 0)
    return jnp.where(row < HEAD_DIM, transposed[:, :EB], transposed[:, EB:])


def attention_kernel(source_ref, count_ref, q_ref, da_ref, kv_ref, *rest):
    att_ref, dq_ref, grads_ref, flipped, scores, sums, qm, qmt, dm, dmt, out_t, dq_t = rest[-12:]
    sources = kv_ref.shape[0]
    blocks = q_ref.shape[0] // EB
    rows_now = UNROLL * TILE
    lane = lax.broadcasted_iota(jnp.int32, (EB, PAIR), 1)
    row = lax.broadcasted_iota(jnp.int32, (PAIR, EB), 0)

    def flip(s, carry):
        for c in range(2):
            flipped[s, c] = kv_ref[s, c].T
        sums[s] = jnp.zeros((2, TILE, PAIR), jnp.float32)
        return carry

    lax.fori_loop(0, sources, flip, 0)

    def spread(block, natural, turned):
        zero = jnp.zeros((EB, PAIR), jnp.bfloat16)
        natural[:EB, :] = jnp.where(lane < HEAD_DIM, block, zero)
        natural[EB:, :] = jnp.where(lane >= HEAD_DIM, block, zero)
        block_t = block.T
        turned[:, :EB] = jnp.where(row < HEAD_DIM, block_t, zero)
        turned[:, EB:] = jnp.where(row >= HEAD_DIM, block_t, zero)

    def one_block(b, carry):
        here = pl.ds(pl.multiple_of(b * EB, EB), EB)
        spread(q_ref[here, :] * jnp.bfloat16(HEAD_DIM**-0.5), qm, qmt)
        spread(da_ref[here, :], dm, dmt)
        count = count_ref[b]
        trips = (count + UNROLL - 1) // UNROLL

        def rows_of(trip):
            return pl.ds(pl.multiple_of(trip * rows_now, rows_now), rows_now)

        def slots_of(trip):
            return [source_ref[b, trip * UNROLL + u] for u in range(UNROLL)]

        def score_step(trip, top):
            for u, slot in enumerate(slots_of(trip)):
                entry = trip * UNROLL + u
                logits = jnp.where(entry < count, dot(kv_ref[slot, 0], qmt[...]), masked_score)
                at = pl.ds(pl.multiple_of(entry * TILE, TILE), TILE)
                scores[at, :] = logits
                top = jnp.maximum(top, jnp.max(logits.reshape(TILE // 8, 8, 2 * EB), axis=0))
            return top

        top = lax.fori_loop(
            0, trips, score_step, jnp.full((8, 2 * EB), masked_score, jnp.float32)
        )
        row_max = jnp.max(top, axis=0, keepdims=True)
        out_t[...] = jnp.zeros_like(out_t)

        def output_step(trip, total):
            at = rows_of(trip)
            terms = jnp.exp(scores[at, :] - row_max)
            scores[at, :] = terms
            values = jnp.concatenate([flipped[s, 1] for s in slots_of(trip)], axis=1)
            out_t[...] += dot(values, terms.astype(jnp.bfloat16))
            return total + jnp.sum(terms.reshape(rows_now // 8, 8, 2 * EB), axis=0)

        total = lax.fori_loop(0, trips, output_step, jnp.zeros((8, 2 * EB), jnp.float32))
        inverse = 1.0 / jnp.sum(total, axis=0, keepdims=True)
        full = out_t[...] * inverse
        att_ref[here, :] = by_head(full).T.astype(jnp.bfloat16)
        delta = jnp.sum(full * dmt[...].astype(jnp.float32), axis=0, keepdims=True)
        dq_t[...] = jnp.zeros_like(dq_t)

        def grad_step(trip, carry):
            at = rows_of(trip)
            slots = slots_of(trip)
            probability = scores[at, :] * inverse
            values = jnp.concatenate([kv_ref[s, 1] for s in slots], axis=0)
            d_weights = dot(values, dmt[...])
            d_scores = (probability * (d_weights - delta)).astype(jnp.bfloat16)
            keys_t = jnp.concatenate([flipped[s, 0] for s in slots], axis=1)
            dq_t[...] += dot(keys_t, d_scores)
            d_keys = dot(d_scores, qm[...])
            d_values = dot(probability.astype(jnp.bfloat16), dm[...])
            for u, slot in enumerate(slots):
                sums[slot, 0] += d_keys[u * TILE : (u + 1) * TILE]
                sums[slot, 1] += d_values[u * TILE : (u + 1) * TILE]
            return carry

        lax.fori_loop(0, trips, grad_step, 0)
        dq_ref[here, :] = (by_head(dq_t[...]).T * HEAD_DIM**-0.5).astype(jnp.bfloat16)
        return carry

    lax.fori_loop(0, blocks, one_block, 0)

    def finish(s, carry):
        grads_ref[s] = sums[s].astype(jnp.bfloat16)
        return carry

    lax.fori_loop(0, sources, finish, 0)


def attention(source, count, queries, d_attended, slots, held, first, pairs):
    sources = slots.shape[0]
    tokens = queries.shape[0]
    entries = source.shape[1]
    columns = pl.BlockSpec((tokens, PAIR), lambda p, *_: (0, first + p))
    chunk = pl.BlockSpec((sources, 2, TILE, PAIR), lambda p, *_: (0, 0, 0, p))
    specs = [columns, columns, chunk]
    operands = [source, count, queries, d_attended, slots]
    aliases = {}
    if held is not None:
        specs += [pl.BlockSpec(memory_space=pl.ANY)] * 2
        operands += list(held)
        aliases = {5: 0, 6: 1}
    whole = jax.ShapeDtypeStruct((tokens, D), jnp.bfloat16)
    products = (tokens // EB) * entries * pairs * TILE * 2 * EB * PAIR * 2 * 6
    return pl.pallas_call(
        attention_kernel,
        grid_spec=pltpu.PrefetchScalarGridSpec(
            num_scalar_prefetch=2,
            grid=(pairs,),
            in_specs=specs,
            out_specs=[columns, columns, chunk],
            scratch_shapes=[
                pltpu.VMEM((sources, 2, TILE, PAIR), jnp.bfloat16),
                pltpu.VMEM((entries * TILE, 2 * EB), jnp.float32),
                pltpu.VMEM((sources, 2, TILE, PAIR), jnp.float32),
                pltpu.VMEM((2 * EB, PAIR), jnp.bfloat16),
                pltpu.VMEM((PAIR, 2 * EB), jnp.bfloat16),
                pltpu.VMEM((2 * EB, PAIR), jnp.bfloat16),
                pltpu.VMEM((PAIR, 2 * EB), jnp.bfloat16),
                pltpu.VMEM((PAIR, 2 * EB), jnp.float32),
                pltpu.VMEM((PAIR, 2 * EB), jnp.float32),
            ],
        ),
        out_shape=[
            whole,
            whole,
            jax.ShapeDtypeStruct((sources, 2, TILE, pairs * PAIR), jnp.bfloat16),
        ],
        input_output_aliases=aliases,
        compiler_params=pltpu.CompilerParams(vmem_limit_bytes=VMEM_LIMIT),
        cost_estimate=pl.CostEstimate(
            flops=products * 4, bytes_accessed=sources * TILE * pairs * PAIR * 8, transcendentals=0
        ),
    )(*operands)


def exchange(array):
    return lax.all_to_all(array, "seq", split_axis=0, concat_axis=0, tiled=True)


def chip_sum(partial, sources):
    core = lax.axis_index("seq") % 2
    parts = partial.reshape(sources // 2, 2, partial.shape[0] // sources, D)
    kept = lax.dynamic_index_in_dim(parts, core, 1, keepdims=False)
    given = lax.dynamic_index_in_dim(parts, 1 - core, 1, keepdims=False).astype(jnp.bfloat16)
    got = lax.ppermute(given, "seq", [(i, i ^ 1) for i in range(sources)])
    return (kept + got.astype(jnp.float32)).astype(jnp.bfloat16)


def chips_sum(chip, sources):
    groups = [list(range(c, sources, 2)) for c in range(2)]
    terms = lax.all_to_all(
        chip, "seq", split_axis=0, concat_axis=0, tiled=True, axis_index_groups=groups
    )
    return jnp.sum(terms.astype(jnp.float32), axis=0)


def local(queries, rgb_kv, tile_ids, tile_count, out_weight, out_grad):
    sources = lax.axis_size("seq")
    tiles_dev = rgb_kv.shape[1] // TILE
    source, request = entry_tables(tile_ids, tile_count, tiles_dev, sources)
    asked = exchange(request[:, None])[:, 0]
    tiles = rgb_kv.reshape(2, tiles_dev, TILE, D)
    starts = [sum(CHUNKS[:i]) for i in range(len(CHUNKS))]
    cuts = list(zip(starts, CHUNKS))
    d_attended = lax.dot_general(
        out_grad, out_weight, (((1,), (1,)), ((), ())), preferred_element_type=jnp.float32
    ).astype(jnp.bfloat16)
    fetched = []
    for first, pairs in cuts:
        outgoing = gather_tiles(asked, tiles, first, pairs)
        if fetched:
            outgoing, d_attended = lax.optimization_barrier((outgoing, d_attended))
        fetched.append(exchange(outgoing))
    held = None
    returned = []
    for (first, pairs), slots in zip(cuts, fetched):
        attended, d_queries, grads = attention(
            source, tile_count, queries, d_attended, slots, held, first, pairs
        )
        if returned:
            attended, grads, returned[-1] = lax.optimization_barrier(
                (attended, grads, returned[-1])
            )
        held = (attended, d_queries)
        returned.append(exchange(grads))
    partial = lax.dot_general(
        attended, out_grad, (((0,), (0,)), ((), ())), preferred_element_type=jnp.float32
    )
    chip = chip_sum(partial, sources)
    chip, returned[-1] = lax.optimization_barrier((chip, returned[-1]))
    d_out_weight = chips_sum(chip, sources)
    joined = dot(attended, out_weight).astype(jnp.bfloat16)
    d_kv = None
    for (first, pairs), terms in zip(cuts, returned):
        d_kv = sum_terms(asked, terms, d_kv, tiles_dev, first, pairs)
    return (joined, d_queries, d_kv.reshape(2, tiles_dev * TILE, D), d_out_weight)


def solution(mesh):
    placed = (
        P(("clip", "seq"), None),
        P("clip", "seq", None),
        P(("clip", "seq"), None),
        P(("clip", "seq")),
        P(),
        P(("clip", "seq"), None),
    )
    return jax.shard_map(
        local,
        mesh=mesh,
        in_specs=placed,
        out_specs=(
            P(("clip", "seq"), None),
            P(("clip", "seq"), None),
            P("clip", "seq", None),
            P(("clip", "seq"), None),
        ),
        check_vma=False,
    )
```

```python
import functools

import jax
import jax.numpy as jnp
from jax import lax
from jax.experimental import pallas as pl
from jax.experimental.pallas import tpu as pltpu
from jax.sharding import PartitionSpec as P

D = 1024
HEADS = 16
EB = 128
TILE = 128
HEAD_DIM = D // HEADS
PAIR = 2 * HEAD_DIM
CHUNKS = (4, 4)
LOTS = 2
VMEM_LIMIT = 48 * 1024 * 1024

masked_score = -1e30


def entry_tables(tile_ids, tile_count, tiles_dev, sources):
    entries = tile_ids.shape[1]
    source = tile_ids // tiles_dev
    within = tile_ids % tiles_dev
    usable = jnp.arange(entries)[None, :] < tile_count[:, None]
    matches = (source[:, :, None] == jnp.arange(sources)[None, None, :]) & usable[:, :, None]
    needed = jnp.any(matches, axis=(0, 1))
    wanted = jnp.max(jnp.where(matches, within[:, :, None], 0), axis=(0, 1))
    request = jnp.where(needed, wanted, -1)
    return (source, request)


def gather_kernel(asked_ref, tiles_ref, out_ref):
    out_ref[0] = tiles_ref[:, 0]


def gather_tiles(asked, tiles, first, pairs):
    sources = asked.shape[0]
    width = pairs * PAIR
    return pl.pallas_call(
        gather_kernel,
        grid_spec=pltpu.PrefetchScalarGridSpec(
            num_scalar_prefetch=1,
            grid=(sources,),
            in_specs=[
                pl.BlockSpec(
                    (2, 1, TILE, width),
                    lambda s, asked_ref: (0, jnp.maximum(asked_ref[s], 0), 0, first // pairs),
                )
            ],
            out_specs=pl.BlockSpec((1, 2, TILE, width), lambda s, asked_ref: (s, 0, 0, 0)),
        ),
        out_shape=jax.ShapeDtypeStruct((sources, 2, TILE, width), jnp.bfloat16),
        compiler_params=pltpu.CompilerParams(vmem_limit_bytes=VMEM_LIMIT),
        cost_estimate=pl.CostEstimate(
            flops=0, bytes_accessed=sources * TILE * width * 8, transcendentals=0
        ),
    )(asked, tiles)


def sum_kernel(asked_ref, terms_ref, *rest):
    out_ref, acc = rest[-2:]
    sources = terms_ref.shape[0]
    acc[...] = jnp.zeros_like(acc)

    def step(s, carry):
        asked = asked_ref[s]

        @pl.when(asked >= 0)
        def _():
            for c in range(2):
                acc[c, asked] += terms_ref[s, c].astype(jnp.float32)

        return carry

    lax.fori_loop(0, sources, step, 0)
    out_ref[...] = acc[...].astype(jnp.bfloat16)


def sum_terms(asked, terms, held, tiles_dev, first, pairs):
    sources = asked.shape[0]
    specs = [
        pl.BlockSpec((sources, 2, TILE, PAIR), lambda p, asked_ref: (0, 0, 0, p)),
    ]
    operands = [asked, terms]
    aliases = {}
    if held is not None:
        specs.append(pl.BlockSpec(memory_space=pl.ANY))
        operands.append(held)
        aliases = {2: 0}
    return pl.pallas_call(
        sum_kernel,
        grid_spec=pltpu.PrefetchScalarGridSpec(
            num_scalar_prefetch=1,
            grid=(pairs,),
            in_specs=specs,
            out_specs=pl.BlockSpec(
                (2, tiles_dev, TILE, PAIR), lambda p, asked_ref: (0, 0, 0, first + p)
            ),
            scratch_shapes=[pltpu.VMEM((2, tiles_dev, TILE, PAIR), jnp.float32)],
        ),
        out_shape=jax.ShapeDtypeStruct((2, tiles_dev, TILE, D), jnp.bfloat16),
        input_output_aliases=aliases,
        compiler_params=pltpu.CompilerParams(vmem_limit_bytes=VMEM_LIMIT),
        cost_estimate=pl.CostEstimate(
            flops=sources * TILE * pairs * PAIR * 2,
            bytes_accessed=sources * TILE * pairs * PAIR * 6,
            transcendentals=0,
        ),
    )(*operands)


def dot(a, b):
    return jnp.dot(a, b, preferred_element_type=jnp.float32)


def by_head(transposed):
    row = lax.broadcasted_iota(jnp.int32, (PAIR, EB), 0)
    return jnp.where(row < HEAD_DIM, transposed[:, :EB], transposed[:, EB:])


def attention_kernel(source_ref, count_ref, q_ref, da_ref, kv_ref, *rest):
    att_ref, dq_ref, grads_ref, flipped, scores, sums, qm_two, qmt_two, dm_two, dmt_two = rest[-10:]
    sources = kv_ref.shape[0]
    blocks = q_ref.shape[0] // EB
    entries = source_ref.shape[1]
    lane = lax.broadcasted_iota(jnp.int32, (EB, PAIR), 1)
    row = lax.broadcasted_iota(jnp.int32, (PAIR, EB), 0)

    def flip(s, carry):
        for c in range(2):
            flipped[s, c] = kv_ref[s, c].T
        sums[s] = jnp.zeros((2, TILE, PAIR), jnp.float32)
        return carry

    lax.fori_loop(0, sources, flip, 0, unroll=4)

    def spread(block, natural, turned):
        zero = jnp.zeros((EB, PAIR), jnp.bfloat16)
        natural[:EB, :] = jnp.where(lane < HEAD_DIM, block, zero)
        natural[EB:, :] = jnp.where(lane >= HEAD_DIM, block, zero)
        block_t = block.T
        turned[:, :EB] = jnp.where(row < HEAD_DIM, block_t, zero)
        turned[:, EB:] = jnp.where(row >= HEAD_DIM, block_t, zero)

    def one_block(b, lot):
        here = pl.ds(pl.multiple_of(b * EB, EB), EB)
        qm, qmt, dm, dmt = (r.at[lot] for r in (qm_two, qmt_two, dm_two, dmt_two))
        spread(q_ref[here, :] * jnp.bfloat16(HEAD_DIM**-0.5), qm, qmt)
        spread(da_ref[here, :], dm, dmt)
        count = count_ref[b]
        slots = [source_ref[b, j] for j in range(entries)]
        top = jnp.full((8, 2 * EB), masked_score, jnp.float32)
        for j, slot in enumerate(slots):
            logits = jnp.where(j < count, dot(kv_ref[slot, 0], qmt[...]), masked_score)
            scores[lot, j * TILE : (j + 1) * TILE, :] = logits
            top = jnp.maximum(top, jnp.max(logits.reshape(TILE // 8, 8, 2 * EB), axis=0))
        row_max = jnp.max(top, axis=0, keepdims=True)
        terms = jnp.exp(scores[lot] - row_max)
        scores[lot] = terms
        values = jnp.concatenate([flipped[s, 1] for s in slots], axis=1)
        out_t = dot(values, terms.astype(jnp.bfloat16))
        inverse = 1.0 / jnp.sum(terms, axis=0, keepdims=True)
        full = out_t * inverse
        att_ref[here, :] = by_head(full).T.astype(jnp.bfloat16)
        delta = jnp.sum(full * dmt[...].astype(jnp.float32), axis=0, keepdims=True)
        probability = scores[lot] * inverse
        d_weights = dot(jnp.concatenate([kv_ref[s, 1] for s in slots], axis=0), dmt[...])
        d_scores = (probability * (d_weights - delta)).astype(jnp.bfloat16)
        dq_t = dot(jnp.concatenate([flipped[s, 0] for s in slots], axis=1), d_scores)
        d_keys = dot(d_scores, qm[...])
        d_values = dot(probability.astype(jnp.bfloat16), dm[...])
        for j, slot in enumerate(slots):
            sums[slot, 0] += d_keys[j * TILE : (j + 1) * TILE]
            sums[slot, 1] += d_values[j * TILE : (j + 1) * TILE]
        dq_ref[here, :] = (by_head(dq_t).T * HEAD_DIM**-0.5).astype(jnp.bfloat16)

    def some_blocks(i, carry):
        for lot in range(LOTS):
            one_block(i * LOTS + lot, lot)
        return carry

    lax.fori_loop(0, blocks // LOTS, some_blocks, 0)

    def finish(s, carry):
        grads_ref[s] = sums[s].astype(jnp.bfloat16)
        return carry

    lax.fori_loop(0, sources, finish, 0, unroll=4)


def attention(source, count, queries, d_attended, slots, held, first, pairs):
    sources = slots.shape[0]
    tokens = queries.shape[0]
    entries = source.shape[1]
    columns = pl.BlockSpec((tokens, PAIR), lambda p, *_: (0, first + p))
    chunk = pl.BlockSpec((sources, 2, TILE, PAIR), lambda p, *_: (0, 0, 0, p))
    specs = [columns, columns, chunk]
    operands = [source, count, queries, d_attended, slots]
    aliases = {}
    if held is not None:
        specs += [pl.BlockSpec(memory_space=pl.ANY)] * 2
        operands += list(held)
        aliases = {5: 0, 6: 1}
    whole = jax.ShapeDtypeStruct((tokens, D), jnp.bfloat16)
    products = (tokens // EB) * entries * pairs * TILE * 2 * EB * PAIR * 2 * 6
    return pl.pallas_call(
        attention_kernel,
        grid_spec=pltpu.PrefetchScalarGridSpec(
            num_scalar_prefetch=2,
            grid=(pairs,),
            in_specs=specs,
            out_specs=[columns, columns, chunk],
            scratch_shapes=[
                pltpu.VMEM((sources, 2, TILE, PAIR), jnp.bfloat16),
                pltpu.VMEM((LOTS, entries * TILE, 2 * EB), jnp.float32),
                pltpu.VMEM((sources, 2, TILE, PAIR), jnp.float32),
                pltpu.VMEM((LOTS, 2 * EB, PAIR), jnp.bfloat16),
                pltpu.VMEM((LOTS, PAIR, 2 * EB), jnp.bfloat16),
                pltpu.VMEM((LOTS, 2 * EB, PAIR), jnp.bfloat16),
                pltpu.VMEM((LOTS, PAIR, 2 * EB), jnp.bfloat16),
            ],
        ),
        out_shape=[
            whole,
            whole,
            jax.ShapeDtypeStruct((sources, 2, TILE, pairs * PAIR), jnp.bfloat16),
        ],
        input_output_aliases=aliases,
        compiler_params=pltpu.CompilerParams(vmem_limit_bytes=VMEM_LIMIT),
        cost_estimate=pl.CostEstimate(
            flops=products * 4, bytes_accessed=sources * TILE * pairs * PAIR * 8, transcendentals=0
        ),
    )(*operands)


def exchange(array):
    return lax.all_to_all(array, "seq", split_axis=0, concat_axis=0, tiled=True)


def chip_sum(partial, sources):
    core = lax.axis_index("seq") % 2
    parts = partial.reshape(sources // 2, 2, partial.shape[0] // sources, D)
    kept = lax.dynamic_index_in_dim(parts, core, 1, keepdims=False)
    given = lax.dynamic_index_in_dim(parts, 1 - core, 1, keepdims=False).astype(jnp.bfloat16)
    got = lax.ppermute(given, "seq", [(i, i ^ 1) for i in range(sources)])
    return (kept + got.astype(jnp.float32)).astype(jnp.bfloat16)


def chips_sum(chip, sources):
    groups = [list(range(c, sources, 2)) for c in range(2)]
    terms = lax.all_to_all(
        chip, "seq", split_axis=0, concat_axis=0, tiled=True, axis_index_groups=groups
    )
    return jnp.sum(terms.astype(jnp.float32), axis=0)


def local(queries, rgb_kv, tile_ids, tile_count, out_weight, out_grad):
    sources = lax.axis_size("seq")
    tiles_dev = rgb_kv.shape[1] // TILE
    source, request = entry_tables(tile_ids, tile_count, tiles_dev, sources)
    asked = exchange(request[:, None])[:, 0]
    tiles = rgb_kv.reshape(2, tiles_dev, TILE, D)
    starts = [sum(CHUNKS[:i]) for i in range(len(CHUNKS))]
    cuts = list(zip(starts, CHUNKS))
    d_attended = lax.dot_general(
        out_grad, out_weight, (((1,), (1,)), ((), ())), preferred_element_type=jnp.float32
    ).astype(jnp.bfloat16)
    fetched = []
    for first, pairs in cuts:
        outgoing = gather_tiles(asked, tiles, first, pairs)
        if fetched:
            outgoing, d_attended = lax.optimization_barrier((outgoing, d_attended))
        fetched.append(exchange(outgoing))
    held = None
    returned = []
    for (first, pairs), slots in zip(cuts, fetched):
        attended, d_queries, grads = attention(
            source, tile_count, queries, d_attended, slots, held, first, pairs
        )
        if returned:
            attended, grads, returned[-1] = lax.optimization_barrier(
                (attended, grads, returned[-1])
            )
        held = (attended, d_queries)
        returned.append(exchange(grads))
    partial = lax.dot_general(
        attended, out_grad, (((0,), (0,)), ((), ())), preferred_element_type=jnp.float32
    )
    chip = chip_sum(partial, sources)
    chip, returned[-1] = lax.optimization_barrier((chip, returned[-1]))
    d_out_weight = chips_sum(chip, sources)
    joined = dot(attended, out_weight).astype(jnp.bfloat16)
    d_kv = None
    for (first, pairs), terms in zip(cuts, returned):
        d_kv = sum_terms(asked, terms, d_kv, tiles_dev, first, pairs)
    return (joined, d_queries, d_kv.reshape(2, tiles_dev * TILE, D), d_out_weight)


def solution(mesh):
    placed = (
        P(("clip", "seq"), None),
        P("clip", "seq", None),
        P(("clip", "seq"), None),
        P(("clip", "seq")),
        P(),
        P(("clip", "seq"), None),
    )
    return jax.shard_map(
        local,
        mesh=mesh,
        in_specs=placed,
        out_specs=(
            P(("clip", "seq"), None),
            P(("clip", "seq"), None),
            P("clip", "seq", None),
            P(("clip", "seq"), None),
        ),
        check_vma=False,
    )
```

```python
import functools

import jax
import jax.numpy as jnp
from jax import lax
from jax.experimental import pallas as pl
from jax.experimental.pallas import tpu as pltpu
from jax.sharding import PartitionSpec as P

D = 1024
HEADS = 16
EB = 128
TILE = 128
HEAD_DIM = D // HEADS
PAIR = 2 * HEAD_DIM
CHUNKS = (4, 4)
LOTS = 2
VMEM_LIMIT = 48 * 1024 * 1024

masked_score = -1e30


def entry_tables(tile_ids, tile_count, tiles_dev, sources):
    entries = tile_ids.shape[1]
    source = tile_ids // tiles_dev
    within = tile_ids % tiles_dev
    usable = jnp.arange(entries)[None, :] < tile_count[:, None]
    matches = (source[:, :, None] == jnp.arange(sources)[None, None, :]) & usable[:, :, None]
    needed = jnp.any(matches, axis=(0, 1))
    wanted = jnp.max(jnp.where(matches, within[:, :, None], 0), axis=(0, 1))
    request = jnp.where(needed, wanted, -1)
    return (source, request)


def gather_kernel(asked_ref, tiles_ref, out_ref):
    out_ref[0] = tiles_ref[:, 0]


def gather_tiles(asked, tiles, first, pairs):
    sources = asked.shape[0]
    width = pairs * PAIR
    return pl.pallas_call(
        gather_kernel,
        grid_spec=pltpu.PrefetchScalarGridSpec(
            num_scalar_prefetch=1,
            grid=(sources,),
            in_specs=[
                pl.BlockSpec(
                    (2, 1, TILE, width),
                    lambda s, asked_ref: (0, jnp.maximum(asked_ref[s], 0), 0, first // pairs),
                )
            ],
            out_specs=pl.BlockSpec((1, 2, TILE, width), lambda s, asked_ref: (s, 0, 0, 0)),
        ),
        out_shape=jax.ShapeDtypeStruct((sources, 2, TILE, width), jnp.bfloat16),
        compiler_params=pltpu.CompilerParams(vmem_limit_bytes=VMEM_LIMIT),
        cost_estimate=pl.CostEstimate(
            flops=0, bytes_accessed=sources * TILE * width * 8, transcendentals=0
        ),
    )(asked, tiles)


def sum_kernel(asked_ref, terms_ref, *rest):
    out_ref, acc = rest[-2:]
    sources = terms_ref.shape[0]
    acc[...] = jnp.zeros_like(acc)

    def step(s, carry):
        asked = asked_ref[s]

        @pl.when(asked >= 0)
        def _():
            for c in range(2):
                acc[c, asked] += terms_ref[s, c].astype(jnp.float32)

        return carry

    lax.fori_loop(0, sources, step, 0)
    out_ref[...] = acc[...].astype(jnp.bfloat16)


def sum_terms(asked, terms, held, tiles_dev, first, pairs):
    sources = asked.shape[0]
    specs = [
        pl.BlockSpec((sources, 2, TILE, PAIR), lambda p, asked_ref: (0, 0, 0, p)),
    ]
    operands = [asked, terms]
    aliases = {}
    if held is not None:
        specs.append(pl.BlockSpec(memory_space=pl.ANY))
        operands.append(held)
        aliases = {2: 0}
    return pl.pallas_call(
        sum_kernel,
        grid_spec=pltpu.PrefetchScalarGridSpec(
            num_scalar_prefetch=1,
            grid=(pairs,),
            in_specs=specs,
            out_specs=pl.BlockSpec(
                (2, tiles_dev, TILE, PAIR), lambda p, asked_ref: (0, 0, 0, first + p)
            ),
            scratch_shapes=[pltpu.VMEM((2, tiles_dev, TILE, PAIR), jnp.float32)],
        ),
        out_shape=jax.ShapeDtypeStruct((2, tiles_dev, TILE, D), jnp.bfloat16),
        input_output_aliases=aliases,
        compiler_params=pltpu.CompilerParams(vmem_limit_bytes=VMEM_LIMIT),
        cost_estimate=pl.CostEstimate(
            flops=sources * TILE * pairs * PAIR * 2,
            bytes_accessed=sources * TILE * pairs * PAIR * 6,
            transcendentals=0,
        ),
    )(*operands)


def dot(a, b):
    return jnp.dot(a, b, preferred_element_type=jnp.float32)


def by_head(transposed):
    row = lax.broadcasted_iota(jnp.int32, (PAIR, EB), 0)
    return jnp.where(row < HEAD_DIM, transposed[:, :EB], transposed[:, EB:])


def attention_kernel(source_ref, count_ref, q_ref, da_ref, kv_ref, *rest):
    att_ref, dq_ref, grads_ref, flipped, scores, sums, qm_two, qmt_two, dm_two, dmt_two = rest[-10:]
    sources = kv_ref.shape[0]
    blocks = q_ref.shape[0] // EB
    entries = source_ref.shape[1]
    lane = lax.broadcasted_iota(jnp.int32, (EB, PAIR), 1)
    row = lax.broadcasted_iota(jnp.int32, (PAIR, EB), 0)

    def flip(s, carry):
        for c in range(2):
            flipped[s, c] = kv_ref[s, c].T
        sums[s] = jnp.zeros((2, TILE, PAIR), jnp.float32)
        return carry

    lax.fori_loop(0, sources, flip, 0, unroll=4)

    def spread(block, natural, turned):
        zero = jnp.zeros((EB, PAIR), jnp.bfloat16)
        natural[:EB, :] = jnp.where(lane < HEAD_DIM, block, zero)
        natural[EB:, :] = jnp.where(lane >= HEAD_DIM, block, zero)
        block_t = block.T
        turned[:, :EB] = jnp.where(row < HEAD_DIM, block_t, zero)
        turned[:, EB:] = jnp.where(row >= HEAD_DIM, block_t, zero)

    def one_block(b, lot):
        here = pl.ds(pl.multiple_of(b * EB, EB), EB)
        qm, qmt, dm, dmt = (r.at[lot] for r in (qm_two, qmt_two, dm_two, dmt_two))
        spread(q_ref[here, :] * jnp.bfloat16(HEAD_DIM**-0.5), qm, qmt)
        spread(da_ref[here, :], dm, dmt)
        count = count_ref[b]
        slots = [source_ref[b, j] for j in range(entries)]
        top = jnp.full((8, 2 * EB), masked_score, jnp.float32)
        for j, slot in enumerate(slots):
            logits = jnp.where(j < count, dot(kv_ref[slot, 0], qmt[...]), masked_score)
            scores[lot, j * TILE : (j + 1) * TILE, :] = logits
            top = jnp.maximum(top, jnp.max(logits.reshape(TILE // 8, 8, 2 * EB), axis=0))
        row_max = jnp.max(top, axis=0, keepdims=True)
        terms = jnp.exp(scores[lot] - row_max)
        scores[lot] = terms
        values = jnp.concatenate([flipped[s, 1] for s in slots], axis=1)
        out_t = dot(values, terms.astype(jnp.bfloat16))
        inverse = 1.0 / jnp.sum(terms, axis=0, keepdims=True)
        full = out_t * inverse
        att_ref[here, :] = by_head(full).T.astype(jnp.bfloat16)
        delta = jnp.sum(full * dmt[...].astype(jnp.float32), axis=0, keepdims=True)
        probability = scores[lot] * inverse
        d_weights = dot(jnp.concatenate([kv_ref[s, 1] for s in slots], axis=0), dmt[...])
        d_scores = (probability * (d_weights - delta)).astype(jnp.bfloat16)
        dq_t = dot(jnp.concatenate([flipped[s, 0] for s in slots], axis=1), d_scores)
        d_keys = dot(d_scores, qm[...])
        d_values = dot(probability.astype(jnp.bfloat16), dm[...])
        for j, slot in enumerate(slots):
            sums[slot, 0] += d_keys[j * TILE : (j + 1) * TILE]
            sums[slot, 1] += d_values[j * TILE : (j + 1) * TILE]
        dq_ref[here, :] = (by_head(dq_t).T * HEAD_DIM**-0.5).astype(jnp.bfloat16)

    def some_blocks(i, carry):
        for lot in range(LOTS):
            one_block(i * LOTS + lot, lot)
        return carry

    lax.fori_loop(0, blocks // LOTS, some_blocks, 0)

    def finish(s, carry):
        grads_ref[s] = sums[s].astype(jnp.bfloat16)
        return carry

    lax.fori_loop(0, sources, finish, 0, unroll=4)


def attention(source, count, queries, d_attended, slots, held, first, pairs):
    sources = slots.shape[0]
    tokens = queries.shape[0]
    entries = source.shape[1]
    columns = pl.BlockSpec((tokens, PAIR), lambda p, *_: (0, first + p))
    chunk = pl.BlockSpec((sources, 2, TILE, PAIR), lambda p, *_: (0, 0, 0, p))
    specs = [columns, columns, chunk]
    operands = [source, count, queries, d_attended, slots]
    aliases = {}
    if held is not None:
        specs += [pl.BlockSpec(memory_space=pl.ANY)] * 2
        operands += list(held)
        aliases = {5: 0, 6: 1}
    whole = jax.ShapeDtypeStruct((tokens, D), jnp.bfloat16)
    products = (tokens // EB) * entries * pairs * TILE * 2 * EB * PAIR * 2 * 6
    return pl.pallas_call(
        attention_kernel,
        grid_spec=pltpu.PrefetchScalarGridSpec(
            num_scalar_prefetch=2,
            grid=(pairs,),
            in_specs=specs,
            out_specs=[columns, columns, chunk],
            scratch_shapes=[
                pltpu.VMEM((sources, 2, TILE, PAIR), jnp.bfloat16),
                pltpu.VMEM((LOTS, entries * TILE, 2 * EB), jnp.float32),
                pltpu.VMEM((sources, 2, TILE, PAIR), jnp.float32),
                pltpu.VMEM((LOTS, 2 * EB, PAIR), jnp.bfloat16),
                pltpu.VMEM((LOTS, PAIR, 2 * EB), jnp.bfloat16),
                pltpu.VMEM((LOTS, 2 * EB, PAIR), jnp.bfloat16),
                pltpu.VMEM((LOTS, PAIR, 2 * EB), jnp.bfloat16),
            ],
        ),
        out_shape=[
            whole,
            whole,
            jax.ShapeDtypeStruct((sources, 2, TILE, pairs * PAIR), jnp.bfloat16),
        ],
        input_output_aliases=aliases,
        compiler_params=pltpu.CompilerParams(vmem_limit_bytes=VMEM_LIMIT),
        cost_estimate=pl.CostEstimate(
            flops=products * 4, bytes_accessed=sources * TILE * pairs * PAIR * 8, transcendentals=0
        ),
    )(*operands)


def exchange(array):
    return lax.all_to_all(array, "seq", split_axis=0, concat_axis=0, tiled=True)


def chip_sum(partial, sources):
    core = lax.axis_index("seq") % 2
    parts = partial.reshape(sources // 2, 2, partial.shape[0] // sources, D)
    kept = lax.dynamic_index_in_dim(parts, core, 1, keepdims=False)
    given = lax.dynamic_index_in_dim(parts, 1 - core, 1, keepdims=False).astype(jnp.bfloat16)
    got = lax.ppermute(given, "seq", [(i, i ^ 1) for i in range(sources)])
    return (kept + got.astype(jnp.float32)).astype(jnp.bfloat16)


def chips_sum(chip, sources):
    chips = sources // 2
    here = lax.axis_index("seq") // 2
    total = lax.dynamic_index_in_dim(chip, here, 0, keepdims=False).astype(jnp.float32)
    for ahead in range(1, chips):
        piece = lax.dynamic_index_in_dim(chip, (here + ahead) % chips, 0, keepdims=False)
        route = [(i, (i // 2 + ahead) % chips * 2 + i % 2) for i in range(sources)]
        total = total + lax.ppermute(piece, "seq", route).astype(jnp.float32)
    return total


def local(queries, rgb_kv, tile_ids, tile_count, out_weight, out_grad):
    sources = lax.axis_size("seq")
    tiles_dev = rgb_kv.shape[1] // TILE
    source, request = entry_tables(tile_ids, tile_count, tiles_dev, sources)
    asked = exchange(request[:, None])[:, 0]
    tiles = rgb_kv.reshape(2, tiles_dev, TILE, D)
    starts = [sum(CHUNKS[:i]) for i in range(len(CHUNKS))]
    cuts = list(zip(starts, CHUNKS))
    d_attended = lax.dot_general(
        out_grad, out_weight, (((1,), (1,)), ((), ())), preferred_element_type=jnp.float32
    ).astype(jnp.bfloat16)
    fetched = []
    for first, pairs in cuts:
        outgoing = gather_tiles(asked, tiles, first, pairs)
        if fetched:
            outgoing, d_attended = lax.optimization_barrier((outgoing, d_attended))
        fetched.append(exchange(outgoing))
    held = None
    returned = []
    for (first, pairs), slots in zip(cuts, fetched):
        attended, d_queries, grads = attention(
            source, tile_count, queries, d_attended, slots, held, first, pairs
        )
        if returned:
            attended, grads, returned[-1] = lax.optimization_barrier(
                (attended, grads, returned[-1])
            )
        held = (attended, d_queries)
        returned.append(exchange(grads))
    partial = lax.dot_general(
        attended, out_grad, (((0,), (0,)), ((), ())), preferred_element_type=jnp.float32
    )
    chip = chip_sum(partial, sources)
    d_out_weight = chips_sum(chip, sources)
    joined = dot(attended, out_weight).astype(jnp.bfloat16)
    d_kv = None
    for (first, pairs), terms in zip(cuts, returned):
        d_kv = sum_terms(asked, terms, d_kv, tiles_dev, first, pairs)
    return (joined, d_queries, d_kv.reshape(2, tiles_dev * TILE, D), d_out_weight)


def solution(mesh):
    placed = (
        P(("clip", "seq"), None),
        P("clip", "seq", None),
        P(("clip", "seq"), None),
        P(("clip", "seq")),
        P(),
        P(("clip", "seq"), None),
    )
    return jax.shard_map(
        local,
        mesh=mesh,
        in_specs=placed,
        out_specs=(
            P(("clip", "seq"), None),
            P(("clip", "seq"), None),
            P("clip", "seq", None),
            P(("clip", "seq"), None),
        ),
        check_vma=False,
    )
```
